32 devices in a mesh: az: 8 (over z, core), tm: 4 (over y, x).
Axes of the slice: x: 2, y: 2, z: 4, core: 2. Of those that a mesh axis runs over, the one named last changes fastest.
Arguments:
- pressure: bfloat16 [16, 64, 64, 4096], P(None, 'az', 'tm'), may hold values from -6 to 6
- offsets: int32 [64, 16], P('tm'), may hold values from -1 to 0
- frac: float32 [64, 16], P('tm'), may hold values from 0 to 1
Outputs:
- csm: float32 [256, 2, 1024, 1024], P('tm', None, 'az')
The draws below stay inside these ranges and needn't reach their ends.
All inputs are finite; a program needn't handle non-finite values.
Results may differ from the reference program's by a relative error of at most 0.0065.
Values may be sent and summed in bfloat16 or wider, within the bound.
A program may use at most 256 MiB of HBM per device.

```python
import math
import jax
import jax.numpy as jnp
from jax import lax

CYCLES = 16
CYCLE_MICS = 64
BLOCK_LEN = 4096
FREQS = 256
SUBS = 16
BLOCKS = 64


def plant(result, key, smallest, top_value):
    extent = result.shape
    place = [jax.random.randint(jax.random.fold_in(key, axis), (), 0, extent[axis]) for axis in range(len(extent))]
    result = result.at[tuple(place)].set(smallest)
    longest = extent.index(max(extent))
    place[longest] = (place[longest] + 1) % extent[longest]
    return result.at[tuple(place)].set(top_value)


def block_scale(key, shape, cuts, smallest, largest):
    loudness, own = 1.0, jax.random.fold_in(key, 6)
    for axis_at, blocks in cuts:
        draws = jnp.exp(jax.random.uniform(jax.random.fold_in(own, axis_at), (blocks,), jnp.float32, smallest / len(cuts), largest / len(cuts)))
        loudness = loudness * jnp.repeat(draws, shape[axis_at] // blocks).reshape([-1 if axis == axis_at else 1 for axis in range(len(shape))])
    return loudness


def normal_values(stream_key, shape, deviation, most, cuts=(), kind=jnp.bfloat16):
    values = jax.random.normal(stream_key, shape, jnp.float32) * deviation
    if len(cuts) > 0:
        values = block_scale(stream_key, shape, cuts, -0.22, 0.18) * values
    return jnp.clip(values, min=-most, max=most).astype(kind)


def setup_inputs(seed: int = 0) -> dict:
    key_list = jax.random.split(jax.random.key(seed), 4)
    pressure = normal_values(key_list[0], (CYCLES, CYCLE_MICS, BLOCKS, BLOCK_LEN), 1.0, 6.0, ((1, 8), (2, 4)))
    offsets = plant(jax.random.randint(key_list[1], (BLOCKS, SUBS), -1, 1), jax.random.fold_in(key_list[1], 1), -1, 0).astype(jnp.int32)
    frac = jnp.clip(1.0 * jax.random.uniform(key_list[2], (BLOCKS, SUBS), jnp.float32) ** block_scale(key_list[2], (BLOCKS, SUBS), ((0, 4),), -0.2, 0.2), 0.0, 1.0)
    return dict(pressure=pressure, offsets=offsets, frac=frac)


def dft_table(length, freqs):
    times = jnp.arange(length, dtype=jnp.int32)
    bins = jnp.arange(1, freqs + 1, dtype=jnp.int32)
    phase = (times[:, None] * bins[None, :] % length).astype(jnp.float32) * (2.0 * math.pi / length)
    hann = 0.5 - 0.5 * jnp.cos(times.astype(jnp.float32) * (2.0 * math.pi / length))
    factor = hann[:, None] / math.sqrt(3.0 * length / 8.0)
    return jnp.concatenate([factor * jnp.cos(phase), -factor * jnp.sin(phase)], axis=1).astype(jnp.bfloat16)

def interp_weights(offsets, frac):
    rows = []
    for shift in range(-1, 2):
        low = (offsets == shift).astype(frac.dtype)
        high = (offsets + 1 == shift).astype(frac.dtype)
        rows.append((1.0 - frac) * low + frac * high)
    return jnp.stack(rows, 0)

def reference(pressure, offsets, frac):
    table = dft_table(BLOCK_LEN, FREQS)
    weights = interp_weights(offsets, frac)
    sub_len = BLOCK_LEN // SUBS

    def one_block(index):
        block = lax.dynamic_index_in_dim(pressure, index, 2, keepdims=False)
        coef = lax.dynamic_index_in_dim(weights, index, 1, keepdims=False)
        total = jnp.zeros((CYCLES, CYCLE_MICS, SUBS, sub_len), jnp.float32)
        for shift in range(-1, 2):
            moved = jnp.roll(block, -shift, axis=1).reshape(CYCLES, CYCLE_MICS, SUBS, sub_len)
            total = total + coef[shift + 1][None, None, :, None] * moved.astype(jnp.float32)
        virtual = total.astype(jnp.bfloat16).reshape(CYCLES * CYCLE_MICS, BLOCK_LEN)
        spec = jnp.dot(virtual, table, preferred_element_type=jnp.float32).astype(jnp.bfloat16)
        return spec.reshape(CYCLES, CYCLE_MICS, 2, FREQS)
    spectra = lax.map(one_block, jnp.arange(BLOCKS, dtype=jnp.int32))
    stacked = spectra.transpose(4, 2, 1, 0, 3).reshape(FREQS, CYCLE_MICS * CYCLES, BLOCKS * 2)

    def one_freq(rows):
        rows32 = rows.astype(jnp.float32)
        split = rows32.reshape(CYCLE_MICS * CYCLES, BLOCKS, 2)
        turned = jnp.stack([split[:, :, 1], -split[:, :, 0]], -1).reshape(CYCLE_MICS * CYCLES, BLOCKS * 2)
        real = jnp.dot(rows32, rows32.T)
        imag = jnp.dot(turned, rows32.T)
        return jnp.stack([real, imag], 0) * (1.0 / BLOCKS)
    return lax.map(one_freq, stacked)
```

```python
import functools
import math

import jax
import jax.numpy as jnp
import numpy as np
from jax import lax
from jax.experimental import pallas as pl
from jax.experimental.pallas import tpu as pltpu
from jax.sharding import PartitionSpec as P

FREQS = 256
LANES = 128
MIB = 1 << 20


def dft_table(length, freqs):
    times = np.arange(length)
    bins = np.arange(1, freqs + 1)
    phase = (times[:, None] * bins[None, :] % length) * (2.0 * math.pi / length)
    hann = 0.5 - 0.5 * np.cos(times * (2.0 * math.pi / length))
    factor = hann[:, None] / math.sqrt(3.0 * length / 8.0)
    table = np.concatenate([factor * np.cos(phase), -factor * np.sin(phase)], axis=1)
    return jnp.asarray(table.astype(jnp.bfloat16))


def interp_weights(offsets, frac):
    rows = []
    for shift in range(-1, 2):
        low = (offsets == shift).astype(frac.dtype)
        high = (offsets + 1 == shift).astype(frac.dtype)
        rows.append((1.0 - frac) * low + frac * high)
    return jnp.stack(rows, 0)


def spread(weight, sub_len):
    blocks, subs = weight.shape
    parts = [
        jnp.broadcast_to(weight[:, s : s + 1], (blocks, sub_len)) for s in range(subs)
    ]
    return parts


def edge_kernel(w_ref, p_ref, table_ref, out_ref, rows_ref):
    cycles, _, blocks, length = p_ref.shape
    subs = w_ref.shape[2]
    sub_len = length // subs
    weight = w_ref[0]
    for s in range(subs):
        cols = pl.ds(s * sub_len, sub_len)
        wide = jnp.broadcast_to(weight[:, s : s + 1], (blocks, sub_len))
        for r in range(cycles):
            rows_ref[pl.ds(r * blocks, blocks), cols] = (
                wide * p_ref[r, 0, :, cols].astype(jnp.float32)
            ).astype(jnp.bfloat16)
    y = jnp.dot(rows_ref[...], table_ref[...], preferred_element_type=jnp.float32)
    for j in range(out_ref.shape[1]):
        out_ref[0, j] = y[:, j * LANES : (j + 1) * LANES].astype(jnp.bfloat16)


def edge_spectra(weights, pressure, table):
    cycles, sector, blocks, length = pressure.shape
    subs = weights.shape[2]
    width = table.shape[1]
    groups = width // LANES
    rows = cycles * blocks
    return pl.pallas_call(
        edge_kernel,
        grid=(2,),
        in_specs=[
            pl.BlockSpec((1, blocks, subs), lambda i: (2 - 2 * i, 0, 0)),
            pl.BlockSpec((cycles, 1, blocks, length), lambda i: (0, (sector - 1) * i, 0, 0)),
            pl.BlockSpec((length, width), lambda i: (0, 0)),
        ],
        out_specs=pl.BlockSpec((1, groups, rows, LANES), lambda i: (i, 0, 0, 0)),
        out_shape=jax.ShapeDtypeStruct((2, groups, rows, LANES), jnp.bfloat16),
        scratch_shapes=[pltpu.VMEM((rows, length), jnp.bfloat16)],
        compiler_params=pltpu.CompilerParams(vmem_limit_bytes=40 * MIB),
        cost_estimate=pl.CostEstimate(
            flops=4 * rows * length * width, bytes_accessed=9 * MIB, transcendentals=0
        ),
    )(weights, pressure, table)


def main_kernel(w_ref, p_ref, table_ref, out_ref, rows_ref):
    count, sector, blocks, length = p_ref.shape
    subs = w_ref.shape[2]
    sub_len = length // subs
    for s in range(subs):
        cols = pl.ds(s * sub_len, sub_len)
        wide = [
            jnp.broadcast_to(w_ref[j, :, s : s + 1], (blocks, sub_len)) for j in range(3)
        ]
        for r in range(count):
            before = None
            here = p_ref[r, 0, :, cols].astype(jnp.float32)
            for m in range(sector):
                after = None
                total = wide[1] * here
                if m > 0:
                    total = total + wide[0] * before
                if m < sector - 1:
                    after = p_ref[r, m + 1, :, cols].astype(jnp.float32)
                    total = total + wide[2] * after
                rows_ref[pl.ds((m * count + r) * blocks, blocks), cols] = total.astype(
                    jnp.bfloat16
                )
                before, here = here, after
    y = jnp.dot(rows_ref[...], table_ref[...], preferred_element_type=jnp.float32)
    for j in range(out_ref.shape[0]):
        out_ref[j] = y[:, j * LANES : (j + 1) * LANES].reshape(sector, count, blocks, LANES)


def main_spectra(weights, pressure, table):
    cycles, sector, blocks, length = pressure.shape
    subs = weights.shape[2]
    width = table.shape[1]
    groups = width // LANES
    count = 4
    return pl.pallas_call(
        main_kernel,
        grid=(cycles // count,),
        in_specs=[
            pl.BlockSpec((3, blocks, subs), lambda i: (0, 0, 0)),
            pl.BlockSpec((count, sector, blocks, length), lambda i: (i, 0, 0, 0)),
            pl.BlockSpec((length, width), lambda i: (0, 0)),
        ],
        out_specs=pl.BlockSpec(
            (groups, sector, count, blocks, LANES), lambda i: (0, 0, i, 0, 0)
        ),
        out_shape=jax.ShapeDtypeStruct((groups, sector, cycles, blocks, LANES), jnp.float32),
        scratch_shapes=[pltpu.VMEM((count * sector * blocks, length), jnp.bfloat16)],
        compiler_params=pltpu.CompilerParams(vmem_limit_bytes=48 * MIB),
        cost_estimate=pl.CostEstimate(
            flops=2 * cycles * sector * blocks * length * width,
            bytes_accessed=24 * MIB,
            transcendentals=0,
        ),
    )(weights, pressure, table)


def turn_kernel(cycles, blocks, y_ref, low_ref, high_ref, out_ref, edge_ref, turned_ref):
    groups, rows, _ = y_ref.shape
    mics = rows // blocks
    edge_ref[0] = low_ref[0].astype(jnp.float32)
    edge_ref[1] = high_ref[0].astype(jnp.float32)
    for j in range(groups):
        half, place = j // (groups // 2), j % (groups // 2)
        for b in range(blocks):
            piece = y_ref[j, pl.ds(b, mics, stride=blocks), :]
            low = edge_ref[0, j, pl.ds(b, cycles, stride=blocks), :]
            high = edge_ref[1, j, pl.ds(b, cycles, stride=blocks), :]
            piece = jnp.concatenate(
                [
                    piece[:cycles] + low,
                    piece[cycles : mics - cycles],
                    piece[mics - cycles :] + high,
                ],
                0,
            )
            first = place * LANES * 2 * blocks + half * blocks + b
            turned_ref[pl.ds(first, LANES, stride=2 * blocks), :] = piece.T
    out_ref[...] = turned_ref[...].astype(jnp.bfloat16)


def turned_spectra(y, low, high, cycles, blocks):
    groups, rows, _ = y.shape
    mics = rows // blocks
    out_rows = groups * LANES * blocks
    edge_rows = cycles * blocks
    return pl.pallas_call(
        functools.partial(turn_kernel, cycles, blocks),
        in_specs=[
            pl.BlockSpec((groups, rows, LANES), lambda: (0, 0, 0)),
            pl.BlockSpec((1, groups, edge_rows, LANES), lambda: (0, 0, 0, 0)),
            pl.BlockSpec((1, groups, edge_rows, LANES), lambda: (0, 0, 0, 0)),
        ],
        out_specs=pl.BlockSpec((out_rows, mics), lambda: (0, 0)),
        out_shape=jax.ShapeDtypeStruct((out_rows, mics), jnp.bfloat16),
        scratch_shapes=[
            pltpu.VMEM((2, groups, edge_rows, LANES), jnp.float32),
            pltpu.VMEM((out_rows, mics), jnp.float32),
        ],
        compiler_params=pltpu.CompilerParams(vmem_limit_bytes=40 * MIB),
    )(y, low, high)


def cross_kernel(blocks, own_ref, all_ref, out_ref):
    count = own_ref.shape[0]
    sectors, _, depth, mics = all_ref.shape
    scale = 1.0 / (depth // 2)
    part = depth // 2 // (depth // (2 * blocks))
    for i in range(count):
        rows = own_ref[i].astype(jnp.float32)
        pieces = []
        for k in range(0, depth, 2 * part):
            pieces.append(rows[k + part : k + 2 * part])
            pieces.append(-rows[k : k + part])
        turned = jnp.concatenate(pieces, 0)
        left = jnp.concatenate([rows.T, turned.T], 0).astype(jnp.bfloat16)
        for a in range(sectors):
            res = jnp.dot(left, all_ref[a, i], preferred_element_type=jnp.float32) * scale
            cols = pl.ds(a * mics, mics)
            out_ref[i, 0, :, cols] = res[:mics]
            out_ref[i, 1, :, cols] = res[mics:]


def cross_spectra(own, every, blocks):
    freqs, depth, mics = own.shape
    sectors = every.shape[0]
    count = 4
    return pl.pallas_call(
        functools.partial(cross_kernel, blocks),
        grid=(freqs // count,),
        in_specs=[
            pl.BlockSpec((count, depth, mics), lambda i: (i, 0, 0)),
            pl.BlockSpec((sectors, count, depth, mics), lambda i: (0, i, 0, 0)),
        ],
        out_specs=pl.BlockSpec((count, 2, mics, sectors * mics), lambda i: (i, 0, 0, 0)),
        out_shape=jax.ShapeDtypeStruct((freqs, 2, mics, sectors * mics), jnp.float32),
        compiler_params=pltpu.CompilerParams(vmem_limit_bytes=40 * MIB),
    )(own, every)


def shards(pressure, offsets, frac):
    cycles, sector, blocks, length = pressure.shape
    table = dft_table(length, FREQS)
    weights = interp_weights(offsets, frac)
    count = lax.axis_size("az")
    forward = [(i, (i + 1) % count) for i in range(count)]
    backward = [(target, source) for source, target in forward]
    edges = edge_spectra(weights, pressure, table)
    high = lax.ppermute(edges[0:1], "az", backward)
    low = lax.ppermute(edges[1:2], "az", forward)
    y = main_spectra(weights, pressure, table)
    y = y.reshape(y.shape[0], sector * cycles * blocks, LANES)
    spectra = turned_spectra(y, low, high, cycles, blocks)
    spectra = spectra.reshape(FREQS, 2 * blocks, sector * cycles)
    own = lax.all_to_all(spectra, "tm", split_axis=0, concat_axis=1, tiled=True)
    every = lax.all_gather(own, "az", axis=0, tiled=False)
    return cross_spectra(own, every, blocks)


def solution(mesh):
    return jax.shard_map(
        shards,
        mesh=mesh,
        in_specs=(P(None, "az", "tm", None), P("tm", None), P("tm", None)),
        out_specs=P("tm", None, "az", None),
        check_vma=False,
    )
```

```python
import functools
import math

import jax
import jax.numpy as jnp
import numpy as np
from jax import lax
from jax.experimental import pallas as pl
from jax.experimental.pallas import tpu as pltpu
from jax.sharding import PartitionSpec as P

FREQS = 256
EIGHTHS = (1, 6, 1)
LANES = 128
MIB = 1 << 20


def dft_table(length, freqs):
    times = np.arange(length)
    bins = np.arange(1, freqs + 1)
    phase = (times[:, None] * bins[None, :] % length) * (2.0 * math.pi / length)
    hann = 0.5 - 0.5 * np.cos(times * (2.0 * math.pi / length))
    factor = hann[:, None] / math.sqrt(3.0 * length / 8.0)
    table = np.concatenate([factor * np.cos(phase), -factor * np.sin(phase)], axis=1)
    return jnp.asarray(table.astype(jnp.bfloat16))


def interp_weights(offsets, frac):
    rows = []
    for shift in range(-1, 2):
        low = (offsets == shift).astype(frac.dtype)
        high = (offsets + 1 == shift).astype(frac.dtype)
        rows.append((1.0 - frac) * low + frac * high)
    return jnp.stack(rows, 0)


def spread(weight, sub_len):
    blocks, subs = weight.shape
    parts = [
        jnp.broadcast_to(weight[:, s : s + 1], (blocks, sub_len)) for s in range(subs)
    ]
    return parts


def edge_kernel(w_ref, p_ref, table_ref, out_ref, rows_ref):
    cycles, _, blocks, length = p_ref.shape
    subs = w_ref.shape[2]
    sub_len = length // subs
    weight = w_ref[0]
    for s in range(subs):
        cols = pl.ds(s * sub_len, sub_len)
        wide = jnp.broadcast_to(weight[:, s : s + 1], (blocks, sub_len))
        for r in range(cycles):
            rows_ref[pl.ds(r * blocks, blocks), cols] = (
                wide * p_ref[r, 0, :, cols].astype(jnp.float32)
            ).astype(jnp.bfloat16)
    y = jnp.dot(rows_ref[...], table_ref[...], preferred_element_type=jnp.float32)
    for j in range(out_ref.shape[1]):
        out_ref[0, j] = y[:, j * LANES : (j + 1) * LANES].astype(jnp.bfloat16)


def edge_spectra(weights, pressure, table):
    cycles, sector, blocks, length = pressure.shape
    subs = weights.shape[2]
    width = table.shape[1]
    groups = width // LANES
    rows = cycles * blocks
    return pl.pallas_call(
        edge_kernel,
        grid=(2,),
        in_specs=[
            pl.BlockSpec((1, blocks, subs), lambda i: (2 - 2 * i, 0, 0)),
            pl.BlockSpec((cycles, 1, blocks, length), lambda i: (0, (sector - 1) * i, 0, 0)),
            pl.BlockSpec((length, width), lambda i: (0, 0)),
        ],
        out_specs=pl.BlockSpec((1, groups, rows, LANES), lambda i: (i, 0, 0, 0)),
        out_shape=jax.ShapeDtypeStruct((2, groups, rows, LANES), jnp.bfloat16),
        scratch_shapes=[pltpu.VMEM((rows, length), jnp.bfloat16)],
        compiler_params=pltpu.CompilerParams(vmem_limit_bytes=40 * MIB),
        cost_estimate=pl.CostEstimate(
            flops=4 * rows * length * width, bytes_accessed=9 * MIB, transcendentals=0
        ),
    )(weights, pressure, table)


def main_kernel(w_ref, p_ref, table_ref, out_ref, rows_ref):
    count, sector, blocks, length = p_ref.shape
    subs = w_ref.shape[2]
    sub_len = length // subs
    for s in range(subs):
        cols = pl.ds(s * sub_len, sub_len)
        wide = [
            jnp.broadcast_to(w_ref[j, :, s : s + 1], (blocks, sub_len)) for j in range(3)
        ]
        for r in range(count):
            before = None
            here = p_ref[r, 0, :, cols].astype(jnp.float32)
            for m in range(sector):
                after = None
                total = wide[1] * here
                if m > 0:
                    total = total + wide[0] * before
                if m < sector - 1:
                    after = p_ref[r, m + 1, :, cols].astype(jnp.float32)
                    total = total + wide[2] * after
                rows_ref[pl.ds((m * count + r) * blocks, blocks), cols] = total.astype(
                    jnp.bfloat16
                )
                before, here = here, after
    y = jnp.dot(rows_ref[...], table_ref[...], preferred_element_type=jnp.float32)
    for j in range(out_ref.shape[0]):
        out_ref[j] = y[:, j * LANES : (j + 1) * LANES].reshape(sector, count, blocks, LANES)


def main_spectra(weights, pressure, table):
    cycles, sector, blocks, length = pressure.shape
    subs = weights.shape[2]
    width = table.shape[1]
    groups = width // LANES
    count = 4
    return pl.pallas_call(
        main_kernel,
        grid=(cycles // count,),
        in_specs=[
            pl.BlockSpec((3, blocks, subs), lambda i: (0, 0, 0)),
            pl.BlockSpec((count, sector, blocks, length), lambda i: (i, 0, 0, 0)),
            pl.BlockSpec((length, width), lambda i: (0, 0)),
        ],
        out_specs=pl.BlockSpec(
            (groups, sector, count, blocks, LANES), lambda i: (0, 0, i, 0, 0)
        ),
        out_shape=jax.ShapeDtypeStruct((groups, sector, cycles, blocks, LANES), jnp.float32),
        scratch_shapes=[pltpu.VMEM((count * sector * blocks, length), jnp.bfloat16)],
        compiler_params=pltpu.CompilerParams(vmem_limit_bytes=48 * MIB),
        cost_estimate=pl.CostEstimate(
            flops=2 * cycles * sector * blocks * length * width,
            bytes_accessed=24 * MIB,
            transcendentals=0,
        ),
    )(weights, pressure, table)


def turn_kernel(cycles, blocks, y_ref, low_ref, high_ref, *refs):
    outs, (edge_ref, turned_ref) = refs[:-2], refs[-2:]
    groups, rows, _ = y_ref.shape
    mics = rows // blocks
    edge_ref[0] = low_ref[0].astype(jnp.float32)
    edge_ref[1] = high_ref[0].astype(jnp.float32)
    for j in range(groups):
        half, place = j // (groups // 2), j % (groups // 2)
        for b in range(blocks):
            piece = y_ref[j, pl.ds(b, mics, stride=blocks), :]
            low = edge_ref[0, j, pl.ds(b, cycles, stride=blocks), :]
            high = edge_ref[1, j, pl.ds(b, cycles, stride=blocks), :]
            piece = jnp.concatenate(
                [
                    piece[:cycles] + low,
                    piece[cycles : mics - cycles],
                    piece[mics - cycles :] + high,
                ],
                0,
            )
            first = place * LANES * 2 * blocks + half * blocks + b
            turned_ref[pl.ds(first, LANES, stride=2 * blocks), :] = piece.T
    first = 0
    for i in range(outs[0].shape[0]):
        for out_ref in outs:
            count = out_ref.shape[1]
            out_ref[i] = turned_ref[pl.ds(first, count), :].astype(jnp.bfloat16)
            first += count


def turned_spectra(y, low, high, cycles, blocks, places):
    groups, rows, _ = y.shape
    mics = rows // blocks
    out_rows = groups * LANES * blocks
    edge_rows = cycles * blocks
    pieces = [(places, out_rows // places * part // 8, mics) for part in EIGHTHS]
    return pl.pallas_call(
        functools.partial(turn_kernel, cycles, blocks),
        in_specs=[
            pl.BlockSpec((groups, rows, LANES), lambda: (0, 0, 0)),
            pl.BlockSpec((1, groups, edge_rows, LANES), lambda: (0, 0, 0, 0)),
            pl.BlockSpec((1, groups, edge_rows, LANES), lambda: (0, 0, 0, 0)),
        ],
        out_specs=[pl.BlockSpec(piece, lambda: (0, 0, 0)) for piece in pieces],
        out_shape=[jax.ShapeDtypeStruct(piece, jnp.bfloat16) for piece in pieces],
        scratch_shapes=[
            pltpu.VMEM((2, groups, edge_rows, LANES), jnp.float32),
            pltpu.VMEM((out_rows, mics), jnp.float32),
        ],
        compiler_params=pltpu.CompilerParams(vmem_limit_bytes=40 * MIB),
    )(y, low, high)


def cross_kernel(blocks, own_ref, all_ref, *refs):
    out_ref = refs[-1]
    count = own_ref.shape[0]
    sectors, _, depth, mics = all_ref.shape
    scale = 1.0 / (depth // 2)
    part = depth // 2 // (depth // (2 * blocks))
    for i in range(count):
        rows = own_ref[i].astype(jnp.float32)
        pieces = []
        for k in range(0, depth, 2 * part):
            pieces.append(rows[k + part : k + 2 * part])
            pieces.append(-rows[k : k + part])
        turned = jnp.concatenate(pieces, 0)
        left = jnp.concatenate([rows.T, turned.T], 0).astype(jnp.bfloat16)
        for a in range(sectors):
            res = jnp.dot(left, all_ref[a, i], preferred_element_type=jnp.float32) * scale
            cols = pl.ds(a * mics, mics)
            out_ref[i, 0, :, cols] = res[:mics]
            out_ref[i, 1, :, cols] = res[mics:]


def cross_spectra(own, every, blocks, first, total, partial):
    freqs, depth, mics = own.shape
    sectors = every.shape[0]
    count = 4
    skip = first // count
    shape = (total, 2, mics, sectors * mics)
    before = [] if partial is None else [partial]
    return pl.pallas_call(
        functools.partial(cross_kernel, blocks),
        grid=(freqs // count,),
        in_specs=[
            pl.BlockSpec((count, depth, mics), lambda i: (i, 0, 0)),
            pl.BlockSpec((sectors, count, depth, mics), lambda i: (0, i, 0, 0)),
        ]
        + [pl.BlockSpec(memory_space=pl.ANY)] * len(before),
        out_specs=pl.BlockSpec(
            (count, 2, mics, sectors * mics), lambda i: (skip + i, 0, 0, 0)
        ),
        out_shape=jax.ShapeDtypeStruct(shape, jnp.float32),
        input_output_aliases={2: 0} if before else {},
        compiler_params=pltpu.CompilerParams(vmem_limit_bytes=40 * MIB),
        cost_estimate=pl.CostEstimate(
            flops=4 * freqs * depth * mics * mics * sectors,
            bytes_accessed=8 * freqs * mics * mics * sectors,
            transcendentals=0,
        ),
    )(own, every, *before)


def shards(pressure, offsets, frac):
    cycles, sector, blocks, length = pressure.shape
    table = dft_table(length, FREQS)
    weights = interp_weights(offsets, frac)
    count = lax.axis_size("az")
    forward = [(i, (i + 1) % count) for i in range(count)]
    backward = [(target, source) for source, target in forward]
    edges = edge_spectra(weights, pressure, table)
    high = lax.ppermute(edges[0:1], "az", backward)
    low = lax.ppermute(edges[1:2], "az", forward)
    y = main_spectra(weights, pressure, table)
    y = y.reshape(y.shape[0], sector * cycles * blocks, LANES)
    places = lax.axis_size("tm")
    pieces = turned_spectra(y, low, high, cycles, blocks, places)
    owned, gathered = [], []
    for piece in pieces:
        piece = piece.reshape(-1, 2 * blocks, sector * cycles)
        own = lax.all_to_all(piece, "tm", split_axis=0, concat_axis=1, tiled=True)
        owned.append(own)
        gathered.append(lax.all_gather(own, "az", axis=0, tiled=False))
    result, first = None, 0
    for own, every in zip(owned, gathered):
        result = cross_spectra(own, every, blocks, first, FREQS // places, result)
        first += own.shape[0]
    return result


def solution(mesh):
    return jax.shard_map(
        shards,
        mesh=mesh,
        in_specs=(P(None, "az", "tm", None), P("tm", None), P("tm", None)),
        out_specs=P("tm", None, "az", None),
        check_vma=False,
    )
```
